32 devices in a mesh: row: 4 (over x, core), col: 8 (over z, y).
Axes of the slice: x: 2, y: 2, z: 4, core: 2. Of those that a mesh axis runs over, the one named last changes fastest.
Arguments:
- field_slab: float32 [672, 8, 4096], P('row', 'col'), may hold values from -16 to 16
- start_basis: float32 [672, 64], replicated, may hold values from -6 to 6
Outputs:
- core_tensor: float32 [64, 8, 4096], P(None, 'col', 'row')
- leading: float32 [672, 64], replicated
The draws below stay inside these ranges and needn't reach their ends.
All inputs are finite; a program needn't handle non-finite values.
Results may differ from the reference program's by a relative error of at most 0.0003.
Values sent between devices are 32-bit elements; how exact they have to be, the bound alone decides.
A program may use at most 64 MiB of HBM per device.

```python
import math
import jax
import jax.numpy as jnp
from jax import lax

N1 = 672
RANK = 64
ITERS = 8
R_DEV = 1024
NY = 8
REST = 4096


def draw_field_slab(key, part):
    subkeys = jax.random.split(key, 6)
    mode_count = 128
    row_groups = REST // R_DEV
    mode_basis = jax.random.normal(subkeys[0], (N1, mode_count), jnp.float32) / math.sqrt(N1)
    amp_second = jnp.exp(jax.random.uniform(subkeys[1], (mode_count, NY), jnp.float32, math.log(0.25), math.log(2.5)))
    amp_third = jnp.exp(jax.random.uniform(subkeys[2], (mode_count, row_groups), jnp.float32, math.log(0.25), math.log(2.5)))
    amp_third = jnp.repeat(amp_third, R_DEV, axis=1)
    weights_mode = jax.random.normal(subkeys[3], (mode_count, NY, REST), jnp.float32)
    weights_mode = weights_mode * amp_second[:, :, None] * amp_third[:, None, :]
    signal_part = jnp.einsum('im,myq->iyq', mode_basis, weights_mode, precision=lax.Precision.HIGHEST)
    noise_part = 0.3 * jax.random.normal(subkeys[4], (N1, NY, REST), jnp.float32)
    row_scale = jnp.exp(jax.random.uniform(subkeys[5], (N1,), jnp.float32, math.log(0.5), math.log(2.0)))
    values = row_scale[:, None, None] * (signal_part + noise_part)
    return jnp.clip(values, -16.0, 16.0)


def gaussian(key, extent, scale, limit, dtype=jnp.bfloat16):
    entries = jax.random.normal(key, extent, jnp.float32) * scale
    return jnp.minimum(jnp.maximum(entries, -limit), limit).astype(dtype)


def setup_inputs(seed: int = 0) -> dict:
    splits = jax.random.split(jax.random.key(seed), 3)
    field_slab = draw_field_slab(jax.random.fold_in(splits[2], 71), 0)
    start_basis = gaussian(splits[1], (N1, RANK), 1.0, 6.0, jnp.float32)
    return {"field_slab": field_slab, "start_basis": start_basis}


def reference(field_slab, start_basis):
    unfolded = field_slab.reshape(N1, NY * REST)
    gram = jnp.dot(unfolded.astype(jnp.float32), unfolded.T.astype(jnp.float32), precision=lax.Precision.HIGHEST, preferred_element_type=jnp.float32)
    leading = start_basis
    for iteration in range(ITERS):
        mapped = jnp.dot(gram.astype(jnp.float32), leading.astype(jnp.float32), precision=lax.Precision.HIGHEST, preferred_element_type=jnp.float32)
        correlation = jnp.dot(mapped.T.astype(jnp.float32), mapped.astype(jnp.float32), precision=lax.Precision.HIGHEST, preferred_element_type=jnp.float32)
        factor = jnp.linalg.cholesky(correlation)
        leading = jax.scipy.linalg.solve_triangular(factor, mapped.T, lower=True).T
    core_tensor = jnp.dot(leading.T.astype(jnp.float32), unfolded.astype(jnp.float32), precision=lax.Precision.HIGHEST, preferred_element_type=jnp.float32)
    return (core_tensor.reshape(RANK, NY, REST), leading)
```

```python
import functools

import jax
import jax.numpy as jnp
from jax import lax
from jax.experimental import pallas as pl
from jax.experimental.pallas import tpu as pltpu
from jax.sharding import PartitionSpec as P

ITERS = 8
HIGHEST = lax.Precision.HIGHEST


def dot(a, b):
    return jnp.dot(a, b, precision=HIGHEST, preferred_element_type=jnp.float32)


def dot_nt(a, b):
    return lax.dot_general(
        a, b, (((1,), (1,)), ((), ())), precision=HIGHEST, preferred_element_type=jnp.float32
    )


def inverse_factor(corr):
    rank = corr.shape[0]
    count = rank // 8
    identity = (
        lax.broadcasted_iota(jnp.int32, (rank, rank), 0)
        == lax.broadcasted_iota(jnp.int32, (rank, rank), 1)
    ).astype(jnp.float32)
    work = jnp.concatenate([corr, identity], axis=1)
    wide = 2 * rank
    rows = [work[8 * i : 8 * i + 8, :] for i in range(count)]
    sub = lax.broadcasted_iota(jnp.int32, (8, wide), 0)
    done = []
    for p in range(count):
        cols = [
            [jnp.broadcast_to(rows[i][:, 8 * p + j : 8 * p + j + 1], (8, wide)) for j in range(8)]
            for i in range(p, count)
        ]
        pivots = jnp.ones((8, wide), jnp.float32)
        for j in range(8):
            pivot = jnp.broadcast_to(cols[0][j][j : j + 1, :], (8, wide))
            pivots = jnp.where(sub == j, pivot, pivots)
            inverse = 1.0 / pivot
            row = jnp.broadcast_to(rows[p][j : j + 1, :], (8, wide))
            upper = {
                m: jnp.broadcast_to(cols[0][m][j : j + 1, :], (8, wide)) for m in range(j + 1, 8)
            }
            for i in range(p, count):
                if i == p and j == 7:
                    continue
                scale = cols[i - p][j] * inverse
                if i == p:
                    scale = jnp.where(sub > j, scale, 0.0)
                for m in range(j + 1, 8):
                    cols[i - p][m] = cols[i - p][m] - scale * upper[m]
                rows[i] = rows[i] - scale * row
        root = lax.rsqrt(pivots)
        root = root * (1.5 - (0.5 * pivots * root) * root)
        done.append((rows[p] * root)[:, rank:])
    return jnp.concatenate(done, axis=0)


def iterate_kernel(gram_ref, start_ref, out_ref, mapped):
    gram = gram_ref[...]
    mapped[...] = dot(start_ref[...].T, gram)

    @pl.loop(0, ITERS - 1)
    def _(step):
        current = mapped[...]
        inverse = inverse_factor(dot_nt(current, current))
        mapped[...] = dot(inverse, dot(current, gram_ref[...]))

    current = mapped[...]
    inverse = inverse_factor(dot_nt(current, current))
    out_ref[...] = dot(inverse, current)


def iterate(gram, start):
    size, rank = start.shape
    return pl.pallas_call(
        iterate_kernel,
        out_shape=jax.ShapeDtypeStruct((rank, size), jnp.float32),
        in_specs=[pl.BlockSpec(memory_space=pltpu.VMEM)] * 2,
        out_specs=pl.BlockSpec(memory_space=pltpu.VMEM),
        scratch_shapes=[pltpu.VMEM((rank, size), jnp.float32)],
        compiler_params=pltpu.CompilerParams(vmem_limit_bytes=32 * 1024 * 1024),
        name="iterate",
    )(gram, start)


def shards(field_slab, start_basis):
    gathered = lax.all_to_all(field_slab, "row", split_axis=2, concat_axis=0, tiled=True)
    flat = gathered.reshape(gathered.shape[0], -1)
    local_gram = dot_nt(flat, flat)
    gram_total = lax.psum(local_gram, ("row", "col"))
    leading_t = iterate(gram_total, start_basis)
    core = dot(leading_t, flat)
    return (core.reshape((-1,) + gathered.shape[1:]), leading_t.T)


def solution(mesh):
    placed = (P("row", "col", None), P())
    return jax.shard_map(
        shards, mesh=mesh, in_specs=placed, out_specs=(P(None, "col", "row"), P()), check_vma=False
    )
```

```python
import functools

import jax
import jax.numpy as jnp
from jax import lax
from jax.experimental import pallas as pl
from jax.experimental.pallas import tpu as pltpu
from jax.sharding import PartitionSpec as P

ITERS = 8
HIGHEST = lax.Precision.HIGHEST


def dot(a, b):
    return jnp.dot(a, b, precision=HIGHEST, preferred_element_type=jnp.float32)


def dot_nt(a, b):
    return lax.dot_general(
        a, b, (((1,), (1,)), ((), ())), precision=HIGHEST, preferred_element_type=jnp.float32
    )


def inverse_factor(corr):
    rank = corr.shape[0]
    count = rank // 8
    identity = (
        lax.broadcasted_iota(jnp.int32, (rank, rank), 0)
        == lax.broadcasted_iota(jnp.int32, (rank, rank), 1)
    ).astype(jnp.float32)
    work = jnp.concatenate([corr, identity], axis=1)
    wide = 2 * rank
    rows = [work[8 * i : 8 * i + 8, :] for i in range(count)]
    sub = lax.broadcasted_iota(jnp.int32, (8, wide), 0)
    done = []
    for p in range(count):
        cols = [
            [jnp.broadcast_to(rows[i][:, 8 * p + j : 8 * p + j + 1], (8, wide)) for j in range(8)]
            for i in range(p, count)
        ]
        pivots = jnp.ones((8, wide), jnp.float32)
        for j in range(8):
            pivot = jnp.broadcast_to(cols[0][j][j : j + 1, :], (8, wide))
            pivots = jnp.where(sub == j, pivot, pivots)
            inverse = 1.0 / pivot
            row = jnp.broadcast_to(rows[p][j : j + 1, :], (8, wide))
            upper = {
                m: jnp.broadcast_to(cols[0][m][j : j + 1, :], (8, wide)) for m in range(j + 1, 8)
            }
            for i in range(p, count):
                if i == p and j == 7:
                    continue
                scale = cols[i - p][j] * inverse
                if i == p:
                    scale = jnp.where(sub > j, scale, 0.0)
                for m in range(j + 1, 8):
                    cols[i - p][m] = cols[i - p][m] - scale * upper[m]
                rows[i] = rows[i] - scale * row
        root = lax.rsqrt(pivots)
        root = root * (1.5 - (0.5 * pivots * root) * root)
        done.append((rows[p] * root)[:, rank:])
    return jnp.concatenate(done, axis=0)


LANES = 128
CHUNK = 256
MESH = pl.DeviceIdType.MESH


def strips(size):
    found, start = [], 0
    for first in range(0, size, LANES):
        width = min(LANES, size - first)
        found.append((first, width, first + width, start))
        start += first + width
    return found, start


def gram_kernel(
    x_size, y_size, z_size, slab_ref, gathered_ref, packed_ref,
    local, total, halves, send, arrive, own, out_sem, rs_send, rs_arrive, ag_send, ag_arrive,
):
    rows, columns = slab_ref.shape
    row_size = 2 * x_size
    width = columns // row_size
    size = rows * row_size
    row, col = lax.axis_index("row"), lax.axis_index("col")
    x, core = row // 2, row % 2
    z, y = col // y_size, col % y_size
    groups = [
        (2, core, lambda i: {"row": x * 2 + i}),
        (x_size, x, lambda i: {"row": i * 2 + core}),
        (y_size, y, lambda i: {"col": z * y_size + i}),
        (z_size, z, lambda i: {"col": i * y_size + y}),
    ]

    barrier = pltpu.get_barrier_semaphore()
    met = 0
    others = [(dx, dc) for dx in range(x_size) for dc in range(2) if dx or dc]
    for dx, dc in others:
        to = ((x + dx) % x_size) * 2 + (core + dc) % 2
        pl.semaphore_signal(barrier, inc=1, device_id={"row": to}, device_id_type=MESH)
        met += 1
    for count, index, place in groups[2:]:
        for k in range(1, count):
            pl.semaphore_signal(
                barrier, inc=1, device_id=place((index + k) % count), device_id_type=MESH
            )
            met += 1
    pl.semaphore_wait(barrier, met)

    chunks = width // CHUNK

    def block_copy(n, chunk):
        dx, dc = others[n]
        to = ((x + dx) % x_size) * 2 + (core + dc) % 2
        return pltpu.make_async_remote_copy(
            src_ref=slab_ref.at[:, pl.ds(pl.multiple_of(to * width + chunk * CHUNK, CHUNK), CHUNK)],
            dst_ref=local.at[
                pl.ds(pl.multiple_of(row * rows, 8), rows),
                pl.ds(pl.multiple_of(chunk * CHUNK, CHUNK), CHUNK),
            ],
            send_sem=send.at[n, chunk],
            recv_sem=arrive.at[n, chunk],
            device_id={"row": to},
            device_id_type=MESH,
        )

    for chunk in range(chunks):
        for n in reversed(range(len(others))):
            block_copy(n, chunk).start()
    mine = pltpu.make_async_copy(
        slab_ref.at[:, pl.ds(pl.multiple_of(row * width, width), width)],
        local.at[pl.ds(pl.multiple_of(row * rows, 8), rows), :],
        own,
    )
    mine.start()
    total[...] = jnp.zeros_like(total)
    mine.wait()
    spans, used = strips(size)

    @pl.loop(0, chunks)
    def _(chunk):
        for n in range(len(others)):
            block_copy(n, chunk).wait_recv()
        part = pl.ds(pl.multiple_of(chunk * CHUNK, CHUNK), CHUNK)
        for first, across, down, start in spans:
            total[start : start + down, 0:across] += dot_nt(
                local[0:down, part], local[first : first + across, part]
            )

    keep = pltpu.make_async_copy(local, gathered_ref, out_sem)
    keep.start()

    length = total.shape[0]
    base = 0
    slot = 0
    at = 0
    bases = []
    for count, index, place in groups:
        piece = length // count
        copies = []
        for k in range(1, count):
            to = (index + k) % count
            copies.append(pltpu.make_async_remote_copy(
                src_ref=total.at[pl.ds(pl.multiple_of(base + to * piece, 8), piece), :],
                dst_ref=halves.at[at + (k - 1) * piece : at + k * piece, :],
                send_sem=rs_send.at[slot + k - 1],
                recv_sem=rs_arrive.at[slot + k - 1],
                device_id=place(to),
                device_id_type=MESH,
            ))
            copies[-1].start()
        for copy in copies:
            copy.wait()
        bases.append((base, slot, length))
        base = base + index * piece
        kept = pl.ds(pl.multiple_of(base, 8), piece)
        value = total[kept, :]
        for k in range(1, count):
            value = value + halves[at + (k - 1) * piece : at + k * piece, :]
        total[kept, :] = value
        at += (count - 1) * piece
        slot += count - 1
        length = piece
    final = pl.ds(pl.multiple_of(base, 8), length)
    packed_ref[final, :] = total[final, :]
    sent = []
    for (count, index, place), (outer, slot, length) in zip(reversed(groups), reversed(bases)):
        piece = length // count
        block = pl.ds(pl.multiple_of(outer + index * piece, 8), piece)
        copies = []
        for k in range(1, count):
            copies.append(pltpu.make_async_remote_copy(
                src_ref=packed_ref.at[block, :],
                dst_ref=packed_ref.at[block, :],
                send_sem=ag_send.at[slot + k - 1],
                recv_sem=ag_arrive.at[slot + k - 1],
                device_id=place((index + k) % count),
                device_id_type=MESH,
            ))
            copies[-1].start()
        for k in range(1, count):
            theirs = pl.ds(pl.multiple_of(outer + ((index - k + count) % count) * piece, 8), piece)
            pltpu.make_async_remote_copy(
                src_ref=packed_ref.at[block, :],
                dst_ref=packed_ref.at[theirs, :],
                send_sem=ag_send.at[slot + k - 1],
                recv_sem=ag_arrive.at[slot + k - 1],
                device_id=place((index + k) % count),
                device_id_type=MESH,
            ).wait_recv()
        sent += copies
    for copy in sent:
        copy.wait_send()

    @pl.loop(0, chunks)
    def _(chunk):
        for n in range(len(others)):
            block_copy(n, chunk).wait_send()

    keep.wait()


def gather_and_gram(slab, row_size, col_size):
    rows, columns = slab.shape
    size, width = rows * row_size, columns // row_size
    devices = row_size * col_size
    packed = strips(size)[1]
    packed = -(-packed // (8 * devices)) * 8 * devices
    x_size, y_size, z_size = row_size // 2, 2, col_size // 2
    steps = (2 - 1) + (x_size - 1) + (y_size - 1) + (z_size - 1)
    dma = pltpu.SemaphoreType.DMA
    return pl.pallas_call(
        functools.partial(gram_kernel, x_size, y_size, z_size),
        out_shape=(
            jax.ShapeDtypeStruct((size, width), jnp.float32),
            jax.ShapeDtypeStruct((packed, LANES), jnp.float32),
        ),
        in_specs=[pl.BlockSpec(memory_space=pl.ANY)],
        out_specs=(pl.BlockSpec(memory_space=pl.ANY), pl.BlockSpec(memory_space=pltpu.VMEM)),
        scratch_shapes=[
            pltpu.VMEM((size, width), jnp.float32),
            pltpu.VMEM((packed, LANES), jnp.float32),
            pltpu.VMEM((packed, LANES), jnp.float32),
            dma((row_size - 1, width // CHUNK)),
            dma((row_size - 1, width // CHUNK)),
            dma(()),
            dma(()),
            dma((steps,)),
            dma((steps,)),
            dma((steps,)),
            dma((steps,)),
        ],
        compiler_params=pltpu.CompilerParams(
            vmem_limit_bytes=40 * 1024 * 1024, collective_id=0, has_side_effects=True
        ),
        name="gather_and_gram",
    )(slab)


def unpack(packed_ref, gram):
    spans, _ = strips(gram.shape[0])
    for first, across, down, start in spans:
        gram[0:down, first : first + across] = packed_ref[start : start + down, 0:across]
        if first:
            gram[first : first + across, 0:first] = packed_ref[start : start + first, 0:across].T


def iterate_kernel(packed_ref, gathered_ref, start_ref, core_ref, out_ref, mapped, gram_ref, gathered, sem):
    fetch = pltpu.make_async_copy(gathered_ref, gathered, sem)
    fetch.start()
    unpack(packed_ref, gram_ref)
    mapped[...] = dot(start_ref[...], gram_ref[...])

    @pl.loop(0, ITERS - 1)
    def _(step):
        current = mapped[...]
        inverse = inverse_factor(dot_nt(current, current))
        mapped[...] = dot(inverse, dot(current, gram_ref[...]))

    current = mapped[...]
    inverse = inverse_factor(dot_nt(current, current))
    leading = dot(inverse, current)
    out_ref[...] = leading
    fetch.wait()
    core_ref[...] = dot(leading, gathered[...])


def iterate(packed, gathered, start):
    rank, size = start.shape
    width = gathered.shape[1]
    vmem = pl.BlockSpec(memory_space=pltpu.VMEM)
    return pl.pallas_call(
        iterate_kernel,
        out_shape=(
            jax.ShapeDtypeStruct((rank, width), jnp.float32),
            jax.ShapeDtypeStruct((rank, size), jnp.float32),
        ),
        in_specs=[vmem, pl.BlockSpec(memory_space=pl.ANY), vmem],
        out_specs=(vmem, vmem),
        scratch_shapes=[
            pltpu.VMEM((rank, size), jnp.float32),
            pltpu.VMEM((size, size), jnp.float32),
            pltpu.VMEM((size, width), jnp.float32),
            pltpu.SemaphoreType.DMA(()),
        ],
        compiler_params=pltpu.CompilerParams(vmem_limit_bytes=40 * 1024 * 1024),
        name="iterate",
    )(packed, gathered, start)


def pack(gram):
    spans, used = strips(gram.shape[0])
    parts = [
        jnp.pad(gram[0:down, first : first + across], ((0, 0), (0, LANES - across)))
        for first, across, down, start in spans
    ]
    return jnp.concatenate(parts, axis=0)


def solution(mesh):
    row_size, col_size = mesh.shape["row"], mesh.shape["col"]

    def shards(field_slab, start_basis):
        rows, depth, columns = field_slab.shape
        slab = field_slab.reshape(rows, depth * columns)
        aligned = depth == 1 and rows % 8 == 0 and row_size % 2 == 0 and col_size % 2 == 0
        if aligned and columns % (row_size * CHUNK) == 0:
            gathered, packed = gather_and_gram(slab, row_size, col_size)
        else:
            gathered = lax.all_to_all(field_slab, "row", split_axis=2, concat_axis=0, tiled=True)
            gathered = gathered.reshape(gathered.shape[0], -1)
            packed = lax.psum(pack(dot_nt(gathered, gathered)), ("row", "col"))
        core, leading_t = iterate(packed, gathered, start_basis.T)
        return (core.reshape(core.shape[0], depth, -1), leading_t.T)

    placed = (P("row", "col", None), P())
    return jax.shard_map(
        shards, mesh=mesh, in_specs=placed, out_specs=(P(None, "col", "row"), P()), check_vma=False
    )
```

```python
import functools

import jax
import jax.numpy as jnp
from jax import lax
from jax.experimental import pallas as pl
from jax.experimental.pallas import tpu as pltpu
from jax.sharding import PartitionSpec as P

ITERS = 8
HIGHEST = lax.Precision.HIGHEST


def dot(a, b):
    return jnp.dot(a, b, precision=HIGHEST, preferred_element_type=jnp.float32)


def dot_nt(a, b):
    return lax.dot_general(
        a, b, (((1,), (1,)), ((), ())), precision=HIGHEST, preferred_element_type=jnp.float32
    )


def inverse_factor(corr):
    rank = corr.shape[0]
    count = rank // 8
    identity = (
        lax.broadcasted_iota(jnp.int32, (rank, rank), 0)
        == lax.broadcasted_iota(jnp.int32, (rank, rank), 1)
    ).astype(jnp.float32)
    work = jnp.concatenate([corr, identity], axis=1)
    wide = 2 * rank
    rows = [work[8 * i : 8 * i + 8, :] for i in range(count)]
    sub = lax.broadcasted_iota(jnp.int32, (8, wide), 0)
    done = []
    for p in range(count):
        cols = [
            [jnp.broadcast_to(rows[i][:, 8 * p + j : 8 * p + j + 1], (8, wide)) for j in range(8)]
            for i in range(p, count)
        ]
        pivots = jnp.ones((8, wide), jnp.float32)
        for j in range(8):
            pivot = jnp.broadcast_to(cols[0][j][j : j + 1, :], (8, wide))
            pivots = jnp.where(sub == j, pivot, pivots)
            inverse = 1.0 / pivot
            row = jnp.broadcast_to(rows[p][j : j + 1, :], (8, wide))
            upper = {
                m: jnp.broadcast_to(cols[0][m][j : j + 1, :], (8, wide)) for m in range(j + 1, 8)
            }
            for i in range(p, count):
                if i == p and j == 7:
                    continue
                scale = cols[i - p][j] * inverse
                if i == p:
                    scale = jnp.where(sub > j, scale, 0.0)
                for m in range(j + 1, 8):
                    cols[i - p][m] = cols[i - p][m] - scale * upper[m]
                rows[i] = rows[i] - scale * row
        root = lax.rsqrt(pivots)
        root = root * (1.5 - (0.5 * pivots * root) * root)
        done.append((rows[p] * root)[:, rank:])
    return jnp.concatenate(done, axis=0)


LANES = 128
CHUNK = 256
MESH = pl.DeviceIdType.MESH


def strips(size):
    found, start = [], 0
    for first in range(0, size, LANES):
        width = min(LANES, size - first)
        found.append((first, width, first + width, start))
        start += first + width
    return found, start


def sizes(half, z_size):
    own = strips(half)[1]
    cross = half * (-(-half // LANES))
    own_unit, cross_unit = 32 * z_size, 64 * z_size
    return -(-own // own_unit) * own_unit, -(-cross // cross_unit) * cross_unit


def remote(source, target, send, arrive, place):
    return pltpu.make_async_remote_copy(
        src_ref=source, dst_ref=target, send_sem=send, recv_sem=arrive,
        device_id=place, device_id_type=MESH,
    )


def reduce_scatter(total, landing, groups, send, arrive):
    length, base, slot, at, levels = total.shape[0], 0, 0, 0, []
    for count, index, place in groups:
        piece = length // count
        copies = []
        for k in range(1, count):
            to = (index + k) % count
            copies.append(remote(
                total.at[pl.ds(pl.multiple_of(base + to * piece, 8), piece), :],
                landing.at[at + (k - 1) * piece : at + k * piece, :],
                send.at[slot + k - 1], arrive.at[slot + k - 1], place(to),
            ))
            copies[-1].start()
        for copy in copies:
            copy.wait()
        levels.append((base, slot, length))
        base = base + index * piece
        kept = pl.ds(pl.multiple_of(base, 8), piece)
        value = total[kept, :]
        for k in range(1, count):
            value = value + landing[at + (k - 1) * piece : at + k * piece, :]
        total[kept, :] = value
        at += (count - 1) * piece
        slot += count - 1
        length = piece
    return base, length, levels


def all_gather(result, offset, groups, levels, send, arrive):
    sent = []
    for (count, index, place), (outer, slot, length) in zip(reversed(groups), reversed(levels)):
        piece = length // count

        def block(i):
            rows = pl.ds(pl.multiple_of(offset + outer + i * piece, 8), piece)
            return result.at[rows, :]

        for k in range(1, count):
            sent.append(remote(
                block(index), block(index), send.at[slot + k - 1], arrive.at[slot + k - 1],
                place((index + k) % count),
            ))
            sent[-1].start()
        for k in range(1, count):
            theirs = block((index - k + count) % count)
            remote(
                theirs, theirs, send.at[slot + k - 1], arrive.at[slot + k - 1],
                place((index + k) % count),
            ).wait_recv()
    return sent


def gram_kernel(
    y_size, z_size, slab_ref, gathered_ref, packed_ref,
    local, extra, own_total, own_landing, cross_total, cross_landing,
    sib_send, sib_arrive, send, arrive, own_sem, out_sem,
    own_rs, own_rs_in, own_ag, own_ag_in, cross_rs, cross_rs_in, cross_ag, cross_ag_in,
    swap, swap_in,
):
    rows, columns = slab_ref.shape
    width, half = columns // 4, 2 * rows
    row, col = lax.axis_index("row"), lax.axis_index("col")
    x, core = row // 2, row % 2
    z, y = col // y_size, col % y_size
    sibling = {"row": x * 2 + 1 - core}
    across_x = {"row": (1 - x) * 2 + core}
    by_core = (2, core, lambda i: {"row": x * 2 + i})
    by_x = (2, x, lambda i: {"row": i * 2 + core})
    by_y = (y_size, y, lambda i: {"col": z * y_size + i})
    by_z = (z_size, z, lambda i: {"col": i * y_size + y})

    barrier = pltpu.get_barrier_semaphore()
    partners = [sibling] + [{"row": (1 - x) * 2 + i} for i in range(2)]
    for count, index, place in (by_y, by_z):
        partners += [place((index + k) % count) for k in range(1, count)]
    for partner in partners:
        pl.semaphore_signal(barrier, inc=1, device_id=partner, device_id_type=MESH)
    pl.semaphore_wait(barrier, len(partners))

    def columns_of(r):
        return slab_ref.at[:, pl.ds(pl.multiple_of(r * width, width), width)]

    my_rows = pl.ds(pl.multiple_of(row * rows, 8), rows)
    my_half_rows = pl.ds(pl.multiple_of(core * rows, 8), rows)
    siblings = [
        remote(columns_of(x * 2 + 1 - core), local.at[my_rows, :],
               sib_send.at[0], sib_arrive.at[0], sibling),
        remote(columns_of((1 - x) * 2 + 1 - core), extra.at[my_half_rows, :],
               sib_send.at[1], sib_arrive.at[1], sibling),
    ]
    chunks = width // CHUNK

    def block_copy(n, chunk):
        to = (1 - x) * 2 + (core + n) % 2
        return remote(
            slab_ref.at[:, pl.ds(pl.multiple_of(to * width + chunk * CHUNK, CHUNK), CHUNK)],
            local.at[my_rows, pl.ds(pl.multiple_of(chunk * CHUNK, CHUNK), CHUNK)],
            send.at[n, chunk], arrive.at[n, chunk], {"row": to},
        )

    for copy in siblings:
        copy.start()
    for chunk in range(chunks):
        for n in range(2):
            block_copy(n, chunk).start()
    mine = [
        pltpu.make_async_copy(columns_of(row), local.at[my_rows, :], own_sem.at[0]),
        pltpu.make_async_copy(
            columns_of((1 - x) * 2 + core), extra.at[my_half_rows, :], own_sem.at[1]
        ),
    ]
    for copy in mine:
        copy.start()
    own_total[...] = jnp.zeros_like(own_total)
    cross_total[...] = jnp.zeros_like(cross_total)
    for copy in mine:
        copy.wait()
    for copy in siblings:
        copy.wait()
    spans, _ = strips(half)

    @pl.loop(0, chunks)
    def _(chunk):
        part = pl.ds(pl.multiple_of(chunk * CHUNK, CHUNK), CHUNK)
        for first, across, down, start in spans:
            upper = pl.ds(pl.multiple_of(x * half, 8), down)
            lower = pl.ds(pl.multiple_of(x * half + first, 8), across)
            own_total[start : start + down, 0:across] += dot_nt(
                local[upper, part], local[lower, part]
            ) + dot_nt(extra[0:down, part], extra[first : first + across, part])

    own_groups = [by_core, by_y, by_z]
    own_size = own_total.shape[0]
    share = own_size // 2
    offset = x * own_size
    base, length, levels = reduce_scatter(own_total, own_landing, own_groups, own_rs, own_rs_in)
    packed_ref[pl.ds(pl.multiple_of(offset + base, 8), length), :] = own_total[
        pl.ds(pl.multiple_of(base, 8), length), :
    ]
    sent = all_gather(packed_ref, offset, own_groups[1:], levels[1:], own_ag, own_ag_in)

    def share_of(i, half_index):
        begin = pl.multiple_of(i * own_size + half_index * share, 8)
        return packed_ref.at[pl.ds(begin, share), :]

    swaps = [
        remote(share_of(x, core), share_of(x, core), swap.at[0], swap_in.at[0], sibling),
        remote(share_of(x, core), share_of(x, core), swap.at[1], swap_in.at[1], across_x),
    ]
    for copy in swaps:
        copy.start()

    @pl.loop(0, chunks)
    def _(chunk):
        for n in range(2):
            block_copy(n, chunk).wait_recv()
        part = pl.ds(pl.multiple_of(chunk * CHUNK, CHUNK), CHUNK)
        for j, (first, across, _, _) in enumerate(spans):
            cross_total[j * half : (j + 1) * half, 0:across] += dot_nt(
                local[0:half, part], local[half + first : half + first + across, part]
            )

    keep = pltpu.make_async_copy(local, gathered_ref, out_sem)
    keep.start()
    cross_groups = [by_core, by_y, by_z, by_x]
    base, length, levels = reduce_scatter(
        cross_total, cross_landing, cross_groups, cross_rs, cross_rs_in
    )
    packed_ref[pl.ds(pl.multiple_of(2 * own_size + base, 8), length), :] = cross_total[
        pl.ds(pl.multiple_of(base, 8), length), :
    ]
    remote(share_of(1 - x, core), share_of(1 - x, core), swap.at[1], swap_in.at[1],
           across_x).wait_recv()
    swaps.append(remote(share_of(1 - x, core), share_of(1 - x, core), swap.at[2], swap_in.at[2],
                        sibling))
    swaps[-1].start()
    sent += all_gather(packed_ref, 2 * own_size, cross_groups, levels, cross_ag, cross_ag_in)
    remote(share_of(x, 1 - core), share_of(x, 1 - core), swap.at[0], swap_in.at[0],
           sibling).wait_recv()
    remote(share_of(1 - x, 1 - core), share_of(1 - x, 1 - core), swap.at[2], swap_in.at[2],
           sibling).wait_recv()
    for copy in sent + swaps:
        copy.wait_send()

    @pl.loop(0, chunks)
    def _(chunk):
        for n in range(2):
            block_copy(n, chunk).wait_send()

    keep.wait()


def gather_and_gram(slab, col_size):
    rows, columns = slab.shape
    half, width = 2 * rows, columns // 4
    y_size, z_size = 2, col_size // 2
    own_size, cross_size = sizes(half, z_size)
    own_steps, cross_steps = 1 + 1 + (z_size - 1), 1 + 1 + (z_size - 1) + 1
    dma = pltpu.SemaphoreType.DMA
    f32 = lambda *shape: pltpu.VMEM(shape, jnp.float32)
    return pl.pallas_call(
        functools.partial(gram_kernel, y_size, z_size),
        out_shape=(
            jax.ShapeDtypeStruct((2 * half, width), jnp.float32),
            jax.ShapeDtypeStruct((2 * own_size + cross_size, LANES), jnp.float32),
        ),
        in_specs=[pl.BlockSpec(memory_space=pl.ANY)],
        out_specs=(pl.BlockSpec(memory_space=pl.ANY), pl.BlockSpec(memory_space=pltpu.VMEM)),
        scratch_shapes=[
            f32(2 * half, width), f32(half, width),
            f32(own_size, LANES), f32(own_size, LANES),
            f32(cross_size, LANES), f32(cross_size, LANES),
            dma((2,)), dma((2,)),
            dma((2, width // CHUNK)), dma((2, width // CHUNK)),
            dma((2,)), dma(()),
        ] + [dma((own_steps,))] * 4 + [dma((cross_steps,))] * 4 + [dma((3,))] * 2,
        compiler_params=pltpu.CompilerParams(
            vmem_limit_bytes=40 * 1024 * 1024, collective_id=0, has_side_effects=True
        ),
        name="gather_and_gram",
    )(slab)


def unpack(packed_ref, gram, half, own_size):
    spans, _ = strips(half)
    padded = gram.shape[0] // 2
    gram[...] = jnp.zeros_like(gram)
    for i in range(2):
        for first, across, down, start in spans:
            at, edge = i * own_size + start, i * padded
            column = edge + first
            gram[edge : edge + down, column : column + LANES] = packed_ref[at : at + down, :]
            if first:
                gram[column : column + LANES, edge : edge + first] = packed_ref[
                    at : at + first, :
                ].T
    for j, (first, _, _, _) in enumerate(spans):
        at, column = 2 * own_size + j * half, padded + first
        block = packed_ref[at : at + half, :]
        gram[0:half, column : column + LANES] = block
        gram[column : column + LANES, 0:half] = block.T


def iterate_kernel(
    own_size, packed_ref, gathered_ref, start_ref, core_ref, out_ref, mapped, gram_ref, gathered, sem
):
    fetch = pltpu.make_async_copy(gathered_ref, gathered, sem)
    fetch.start()
    rank, size = start_ref.shape
    half, padded = size // 2, gram_ref.shape[0] // 2
    unpack(packed_ref, gram_ref, half, own_size)
    gap = jnp.zeros((rank, padded - half), jnp.float32)
    start = start_ref[...]
    start = jnp.concatenate([start[:, :half], gap, start[:, half:], gap], axis=1)
    mapped[...] = dot(start, gram_ref[...])

    @pl.loop(0, ITERS - 1)
    def _(step):
        current = mapped[...]
        inverse = inverse_factor(dot_nt(current, current))
        mapped[...] = dot(inverse, dot(current, gram_ref[...]))

    current = mapped[...]
    inverse = inverse_factor(dot_nt(current, current))
    leading = dot(inverse, current)
    leading = jnp.concatenate([leading[:, :half], leading[:, padded : padded + half]], axis=1)
    out_ref[...] = leading
    fetch.wait()
    core_ref[...] = dot(leading, gathered[...])


def iterate(packed, gathered, start, own_size):
    rank, size = start.shape
    width = gathered.shape[1]
    padded = 2 * LANES * (-(-size // (2 * LANES)))
    vmem = pl.BlockSpec(memory_space=pltpu.VMEM)
    return pl.pallas_call(
        functools.partial(iterate_kernel, own_size),
        out_shape=(
            jax.ShapeDtypeStruct((rank, width), jnp.float32),
            jax.ShapeDtypeStruct((rank, size), jnp.float32),
        ),
        in_specs=[vmem, pl.BlockSpec(memory_space=pl.ANY), vmem],
        out_specs=(vmem, vmem),
        scratch_shapes=[
            pltpu.VMEM((rank, padded), jnp.float32),
            pltpu.VMEM((padded, padded), jnp.float32),
            pltpu.VMEM((size, width), jnp.float32),
            pltpu.SemaphoreType.DMA(()),
        ],
        compiler_params=pltpu.CompilerParams(vmem_limit_bytes=40 * 1024 * 1024),
        name="iterate",
    )(packed, gathered, start)


def pack(gram, own_size, cross_size):
    half = gram.shape[0] // 2
    spans, used = strips(half)
    wide = lambda part, across: jnp.pad(part, ((0, 0), (0, LANES - across)))
    parts = []
    for i in range(2):
        own = gram[i * half : (i + 1) * half, i * half : (i + 1) * half]
        parts += [wide(own[0:down, a : a + w], w) for a, w, down, _ in spans]
        parts.append(jnp.zeros((own_size - used, LANES), jnp.float32))
    cross = gram[:half, half:]
    parts += [wide(cross[:, a : a + w], w) for a, w, _, _ in spans]
    parts.append(jnp.zeros((cross_size - half * len(spans), LANES), jnp.float32))
    return jnp.concatenate(parts, axis=0)


def solution(mesh):
    row_size, col_size = mesh.shape["row"], mesh.shape["col"]

    def shards(field_slab, start_basis):
        rows, depth, columns = field_slab.shape
        slab = field_slab.reshape(rows, depth * columns)
        own_size, cross_size = sizes(rows * row_size // 2, col_size // 2)
        aligned = depth == 1 and rows % 8 == 0 and row_size == 4 and col_size % 2 == 0
        if aligned and columns % (row_size * CHUNK) == 0:
            gathered, packed = gather_and_gram(slab, col_size)
        else:
            gathered = lax.all_to_all(field_slab, "row", split_axis=2, concat_axis=0, tiled=True)
            gathered = gathered.reshape(gathered.shape[0], -1)
            packed = pack(dot_nt(gathered, gathered), own_size, cross_size)
            packed = lax.psum(packed, ("row", "col"))
        core, leading_t = iterate(packed, gathered, start_basis.T, own_size)
        return (core.reshape(core.shape[0], depth, -1), leading_t.T)

    placed = (P("row", "col", None), P())
    return jax.shard_map(
        shards, mesh=mesh, in_specs=placed, out_specs=(P(None, "col", "row"), P()), check_vma=False
    )
```
